512 devices in a mesh: section: 64 (over z, y_lo, core), tensor: 8 (over x, y_hi).
Axes of the slice: x: 4, y: 4 (y_hi: 2, y_lo: 2; y = y_hi * 2 + y_lo), z: 16, core: 2. Of those that a mesh axis runs over, the one named last changes fastest.
Arguments:
- state_coef: bfloat16 [64, 384, 512], P('section'), may hold values from -12 to 12
- embed_terms: bfloat16 [64, 2, 384, 8192], P('section', None, None, 'tensor'), may hold values from -4 to 4
- norm_gain: bfloat16 [64, 8192], P('section', 'tensor'), may hold values from 0.099609375 to 1.8984375
- w_query: bfloat16 [64, 8192, 512], P('section', 'tensor'), may hold values from -0.055242717 to 0.055242717
- w_keyval: bfloat16 [64, 8192, 256], P('section', 'tensor'), may hold values from -0.055242717 to 0.055242717
- w_out: bfloat16 [64, 512, 8192], P('section', None, 'tensor'), may hold values from -0.25 to 0.25
- basis: bfloat16 [8192, 512], P('tensor'), may hold values from -0.0625 to 0.0625
- doc_lengths: int32 [64, 2, 4], P('section'), may hold values from 1 to 192, 384 in all within a row
Outputs:
- boundary: bfloat16 [64, 2, 384, 512], P('section')
The draws below stay inside these ranges and needn't reach their ends.
Inputs may be any that keep to these rules, and one draw needn't show every extreme that they name: `doc_lengths`: each row holds 4 lengths summing to 384; its largest is 192.
All inputs are finite; a program needn't handle non-finite values.
Results may differ from the reference program's by a relative error of at most 0.007.
Values may be sent and summed in bfloat16 or wider, within the bound.
No kernel may reach another device: no remote copies, remote signals or barrier semaphores. Data moves between devices by JAX's collectives and lax.ppermute only.
A program may use at most 64 MiB of HBM per device.

```python
import math
import jax
import jax.numpy as jnp
import numpy as np
from jax import lax

D = 8192
HEAD = 128
GROUP = 4
R = 512
S = 384
TICKS = 2
DOCS = 4
SECTIONS = 64


def draw_embed_terms(key, part):
    key = jax.random.fold_in(key, 5)
    base = jax.random.normal(key, (SECTIONS, TICKS, S, D), jnp.float32) * 0.5
    return jnp.clip(base, -4.0, 4.0).astype(jnp.bfloat16)


def draw_w_query(key, part):
    key = jax.random.fold_in(key, 3)
    limit = 4.5 * D ** (-0.5)
    base = jax.random.normal(key, (SECTIONS, D, GROUP * HEAD), jnp.float32) * D ** (-0.5)
    return jnp.clip(base, -limit, limit).astype(jnp.bfloat16)


def draw_w_keyval(key, part):
    key = jax.random.fold_in(key, 4)
    limit = 4.5 * D ** (-0.5)
    base = jax.random.normal(key, (SECTIONS, D, 2 * HEAD), jnp.float32) * D ** (-0.5)
    return jnp.clip(base, -limit, limit).astype(jnp.bfloat16)


def block_scale(key, shape, cuts, low, largest):
    loudness = 1.0
    for dim, shards_of in cuts:
        heights = jax.random.uniform(jax.random.fold_in(jax.random.fold_in(key, 6), dim), (shards_of,), jnp.float32, low / len(cuts), largest / len(cuts))
        loudness = loudness * jnp.repeat(jnp.exp(heights), shape[dim] // shards_of).reshape((-1,) + (1,) * (len(shape) - 1 - dim))
    return loudness


def profile(amount, total, reach, lean):
    loads = [(1 << 20) // math.isqrt(rank ** lean) + 1 for rank in range(2, amount + 1)]
    spare, holding = total - reach - (amount - 1), [1] * (amount - 1)
    while spare > 0:
        movable = [i for i in range(amount - 1) if holding[i] < reach]
        pool, left = sum([loads[i] for i in movable]), spare
        for i in movable:
            extra = min(reach - holding[i], max(1, left * loads[i] // pool), spare)
            holding[i] = holding[i] + extra
            spare = spare - extra
    return np.array([reach] + holding)


def ragged(key, number_of, total, most, skew):
    if number_of == 2:
        one = jax.random.randint(key, (), max(1, total - most), min(most, total - 1) + 1)
        return jnp.stack([one, total - one])
    sizes = jnp.asarray(profile(number_of, total, most, skew), jnp.int32)
    pairs = (number_of - 1) // 2
    source_of, taker = sizes[1:1 + 2 * pairs:2], sizes[2:2 + 2 * pairs:2]
    slack = jnp.minimum(source_of - 1, most - taker)
    shifted = jax.random.randint(jax.random.fold_in(key, 1), (pairs,), 0, 1 << 20) % (slack + 1)
    sizes = sizes.at[1:1 + 2 * pairs:2].set(source_of - shifted).at[2:2 + 2 * pairs:2].set(taker + shifted)
    return sizes[jax.random.permutation(jax.random.fold_in(key, 2), number_of)]


def bell_draw(stream_key, dims, scale, most, shards=(), kind=jnp.bfloat16):
    array = scale * jax.random.normal(stream_key, dims, jnp.float32)
    if shards:
        array = array * block_scale(stream_key, dims, shards, -0.22, 0.18)
    return jnp.clip(array, -most, most).astype(kind)


def setup_inputs(seed: int = 0) -> dict:
    seeds = jax.random.split(jax.random.key(seed), 9)
    state_coef = bell_draw(seeds[0], (SECTIONS, S, R), 2.0, 12.0, ((0, 64),))
    embed_terms = draw_embed_terms(jax.random.fold_in(seeds[8], 71), 0)
    norm_gain = jnp.clip(1.0 + 0.18 * jax.random.normal(seeds[2], (SECTIONS, D), jnp.float32), 0.099609375, 1.8984375).astype(jnp.bfloat16)
    w_query = draw_w_query(jax.random.fold_in(seeds[8], 71), 0)
    w_keyval = draw_w_keyval(jax.random.fold_in(seeds[8], 71), 0)
    w_out = bell_draw(seeds[5], (SECTIONS, GROUP * HEAD, D), (GROUP * HEAD) ** -0.5, 0.25, ((0, 64), (2, 8)))
    basis = bell_draw(seeds[6], (D, R), D ** -0.5, 0.0625, ((0, 8),))
    doc_lengths = jax.vmap(lambda own: ragged(own, DOCS, S, S // 2, 2))(jax.random.split(seeds[7], SECTIONS * TICKS)).reshape((SECTIONS, TICKS, DOCS)).astype(jnp.int32)
    return {"state_coef": state_coef, "embed_terms": embed_terms, "norm_gain": norm_gain, "w_query": w_query, "w_keyval": w_keyval, "w_out": w_out, "basis": basis, "doc_lengths": doc_lengths}


def doc_layout(lengths, length_total):
    indices = jnp.arange(length_total, dtype=jnp.int32)
    doc_ends = jnp.cumsum(lengths).astype(jnp.int32)
    segment = lax.optimization_barrier(jnp.sum((indices[:, None] >= doc_ends[None, :]).astype(jnp.int32), axis=1)).astype(jnp.int32)
    starts = doc_ends - lengths
    chosen = segment[:, None] == jnp.arange(lengths.shape[0], dtype=jnp.int32)[None, :]
    begin = lax.optimization_barrier(jnp.sum(jnp.where(chosen, starts[None, :], 0), axis=1)).astype(jnp.int32)
    return (segment, (indices - begin).astype(jnp.float32))

def rotate_heads(block, position):
    half_head = HEAD // 2
    frequency = 500000.0 ** (-(jnp.arange(half_head, dtype=jnp.float32) * 2.0) / HEAD)
    angles = position[:, None, None] * frequency[None, None, :]
    cosine = jnp.cos(angles)
    sine_part = jnp.sin(angles)
    first_half = block[..., :half_head]
    second_half = block[..., half_head:]
    return jnp.concatenate([first_half * cosine - second_half * sine_part, second_half * cosine + first_half * sine_part], axis=-1)

def embed_positions(block, position):
    count_rows = block.shape[0]
    width_q = GROUP * HEAD
    queries = rotate_heads(block[:, :width_q].reshape(count_rows, GROUP, HEAD), position)
    key_head = rotate_heads(block[:, width_q:width_q + HEAD].reshape(count_rows, 1, HEAD), position)
    return jnp.concatenate([queries.reshape(count_rows, width_q), key_head.reshape(count_rows, HEAD), block[:, width_q + HEAD:]], axis=1).astype(jnp.bfloat16)

def attend(combined, segment):
    count_rows = combined.shape[0]
    width_q = GROUP * HEAD
    queries = combined[:, :width_q].reshape(count_rows, GROUP, HEAD).astype(jnp.float32)
    keys = combined[:, width_q:width_q + HEAD].astype(jnp.float32)
    values = combined[:, width_q + HEAD:].astype(jnp.float32)
    scores = jnp.einsum('sgh,th->gst', queries, keys) * HEAD ** (-0.5)
    indices = jnp.arange(count_rows, dtype=jnp.int32)
    allowed = (segment[:, None] == segment[None, :]) & (indices[None, :] <= indices[:, None])
    scores = jnp.where(allowed[None], scores, -1e+30)
    peak = lax.optimization_barrier(jnp.max(scores, axis=-1, keepdims=True))
    expo = jnp.exp(scores - peak)
    weights = (expo / lax.optimization_barrier(jnp.sum(expo, axis=-1, keepdims=True))).astype(jnp.bfloat16)
    result = jnp.einsum('gst,th->sgh', weights.astype(jnp.float32), values)
    return result.reshape(count_rows, width_q).astype(jnp.bfloat16)

def section_layer(coef_in, embedded, gain_row, w_q, w_kv, w_o, lengths, basis):
    lifted = jnp.dot(coef_in, basis.T, preferred_element_type=jnp.float32)
    stream = embedded.astype(jnp.float32) + lifted
    inverse = lax.rsqrt(lax.optimization_barrier(jnp.mean(stream * stream, axis=-1, keepdims=True)) + 1e-05)
    normed = (stream * inverse * gain_row.astype(jnp.float32)).astype(jnp.bfloat16)
    queries = jnp.dot(normed, w_q, preferred_element_type=jnp.float32)
    keyval = jnp.dot(normed, w_kv, preferred_element_type=jnp.float32)
    segment, position = doc_layout(lengths, coef_in.shape[0])
    combined = embed_positions(jnp.concatenate([queries, keyval], axis=1), position)
    attended = attend(combined, segment)
    attn_out = jnp.dot(attended, w_o, preferred_element_type=jnp.float32)
    carried = (lifted + attn_out).astype(jnp.bfloat16)
    return jnp.dot(carried, basis, preferred_element_type=jnp.float32).astype(jnp.bfloat16)

def reference(state_coef, embed_terms, norm_gain, w_query, w_keyval, w_out, basis, doc_lengths):
    coef_now = state_coef
    produced = []
    for step_index in range(TICKS):

        def section_step(items):
            return section_layer(items[0], items[1], items[2], items[3], items[4], items[5], items[6], basis)
        section_out = lax.map(section_step, (coef_now, embed_terms[:, step_index], norm_gain, w_query, w_keyval, w_out, doc_lengths[:, step_index]))
        produced.append(section_out)
        coef_now = jnp.concatenate([jnp.zeros_like(section_out[:1]), section_out[:-1]], axis=0)
    return jnp.stack(produced, axis=1)
```

```python
import functools
import math

import jax
import jax.numpy as jnp
from jax import lax
from jax.experimental import pallas as pl
from jax.experimental.pallas import tpu as pltpu
from jax.sharding import PartitionSpec as P

HEAD = 128
GROUP = 4
WIDTH_Q = GROUP * HEAD
WIDTH = WIDTH_Q + 2 * HEAD
PARTS = 8
ROWS = 384
OWN = ROWS // PARTS
RANK = 512
PANEL = 256
M_OWN = RANK // PARTS
G_OWN = HEAD // PARTS
BF16 = jnp.bfloat16
F32 = jnp.float32
MIB = 1024 * 1024
LIMIT0 = 56

QKV_ROWS = OWN * (WIDTH // HEAD)
M_AT = QKV_ROWS
G_AT = M_AT + M_OWN * (RANK // HEAD)
G_BLOCKS = ((0, 0), (0, 1), (1, 1), (2, 2), (2, 3), (3, 3), (0, 2), (0, 3), (1, 2), (1, 3))
MIXED_ROWS = G_AT + len(G_BLOCKS) * G_OWN
TAIL = 16

VMEM = pl.BlockSpec(memory_space=pltpu.VMEM)
SMEM = pl.BlockSpec(memory_space=pltpu.SMEM)
ANY = pl.BlockSpec(memory_space=pl.ANY)
HBM = pl.BlockSpec(memory_space=pltpu.HBM)


def call(body, name, out_shape, in_specs, flops, moved, args, scratch=(), out_specs=VMEM, limit=16):
    return pl.pallas_call(
        body,
        name=name,
        out_shape=out_shape,
        in_specs=in_specs,
        out_specs=out_specs,
        scratch_shapes=scratch,
        cost_estimate=pl.CostEstimate(flops=flops, bytes_accessed=moved, transcendentals=0),
        compiler_params=pltpu.CompilerParams(vmem_limit_bytes=limit * MIB),
    )(*args)


def dot(a, b):
    return jnp.dot(a, b, preferred_element_type=F32)


def dot_t(a, b):
    return lax.dot_general(a, b, (((1,), (1,)), ((), ())), preferred_element_type=F32)


def column_to_row(column):
    shape = (column.shape[0], HEAD)
    row = lax.broadcasted_iota(jnp.int32, shape, 0)
    lane = lax.broadcasted_iota(jnp.int32, shape, 1)
    return jnp.sum(jnp.where(row == lane, column, 0.0), axis=0, keepdims=True)


def row_to_column(row_vector, rows):
    row = lax.broadcasted_iota(jnp.int32, (rows, HEAD), 0)
    lane = lax.broadcasted_iota(jnp.int32, (rows, HEAD), 1)
    return jnp.sum(jnp.where(row == lane, row_vector, 0.0), axis=1, keepdims=True)


def pack(out, value, at, rows):
    for column in range(value.shape[1] // HEAD):
        part = value[:, column * HEAD : (column + 1) * HEAD]
        for to in range(PARTS):
            out[to, at + column * rows : at + (column + 1) * rows, :] = part[
                to * rows : (to + 1) * rows
            ]


def unpack(packed, at, rows, columns=1):
    parts = [
        packed[:, at + column * rows : at + (column + 1) * rows, :].reshape(PARTS * rows, HEAD)
        for column in range(columns)
    ]
    return parts[0] if columns == 1 else jnp.concatenate(parts, axis=1)


def qkv_sums(stream, squares, gain, weights, ready, buffer):
    tail_at = buffer.shape[1] - TAIL
    scaled = (stream * gain.astype(F32)).astype(BF16)
    row = lax.broadcasted_iota(jnp.int32, (TAIL, HEAD), 0)
    for to in range(PARTS):
        laid = column_to_row(squares[to * OWN : (to + 1) * OWN])
        high = laid.astype(BF16).astype(F32)
        value = jnp.where(row == 0, high, jnp.where(row == 1, laid - high, 0.0))
        buffer[to, tail_at:, :] = value.astype(BF16)
    ready()
    w_q, w_kv = weights
    for panel in range(WIDTH // PANEL):
        if panel < WIDTH_Q // PANEL:
            weight = w_q[:, panel * PANEL : (panel + 1) * PANEL]
        else:
            weight = w_kv[...]
        pack(buffer, dot(scaled, weight).astype(BF16), panel * OWN * (PANEL // HEAD), OWN)


def rotary_tables(lengths, tables):
    lane = lax.broadcasted_iota(jnp.int32, (OWN, HEAD), 1)
    half = HEAD // 2
    pair = jnp.where(lane < half, lane, lane - half).astype(F32)
    frequency = jnp.exp(pair * (-math.log(500000.0) / half))
    index = lax.broadcasted_iota(jnp.int32, (OWN, HEAD), 0) + lax.axis_index("tensor") * OWN
    for step in range(2):
        end, begin = 0, jnp.zeros((OWN, HEAD), jnp.int32)
        for document in range(3):
            end = end + lengths[0, step, document]
            begin = jnp.where(index >= end, end, begin)
        angle = (index - begin).astype(F32) * frequency
        sine = jnp.sin(angle)
        tables[2 * step] = jnp.cos(angle)
        tables[2 * step + 1] = jnp.where(lane < half, -sine, sine)


def symmetric_sums(basis, buffer):
    left, right = basis[:, :PANEL], basis[:, PANEL:]
    turned = left.T
    parts = {
        (0, 0): dot(turned, left).astype(BF16),
        (0, 2): dot(turned, right).astype(BF16),
        (2, 2): dot(right.T, right).astype(BF16),
    }
    for place, (row, column) in enumerate(G_BLOCKS):
        part = parts[(row // 2 * 2, column // 2 * 2)]
        row, column = row % 2 * HEAD, column % 2 * HEAD
        block = part[row : row + HEAD, column : column + HEAD]
        pack(buffer, block, G_AT + place * G_OWN, G_OWN)


def symmetric_blocks(packed):
    blocks = {
        pair: unpack(packed, G_AT + place * G_OWN, G_OWN) for place, pair in enumerate(G_BLOCKS)
    }

    def part(row, column):
        corner = (
            blocks[(row + 1, column)] if row != column else blocks[(row, column + 1)].T
        )
        upper = jnp.concatenate([blocks[(row, column)], blocks[(row, column + 1)]], axis=1)
        lower = jnp.concatenate([corner, blocks[(row + 1, column + 1)]], axis=1)
        return jnp.concatenate([upper, lower], axis=0)

    return part(0, 0), part(0, 2), part(2, 2)


def project0_kernel(
    lengths_in, basis_in, wo_in, coef_in, emb_in, gain_in, wq_in, wkv_in, out, tables,
    lengths, basis, w_o, coef, emb, gain, w_q, w_kv, sems,
):
    pairs = [
        (lengths_in, lengths), (basis_in, basis), (wo_in, w_o), (coef_in, coef),
        (emb_in.at[0, 0], emb), (gain_in, gain), (wq_in, w_q), (wkv_in, w_kv),
    ]
    copies = [
        pltpu.make_async_copy(source, target, sems.at[i])
        for i, (source, target) in enumerate(pairs)
    ]
    for copy in copies[:3]:
        copy.start()
    copies[0].wait()
    for copy in copies[3:]:
        copy.start()
    rotary_tables(lengths, tables)
    copies[1].wait()
    copies[2].wait()
    pack(out, dot(w_o[...], basis[...]).astype(BF16), M_AT, M_OWN)
    symmetric_sums(basis, out)
    for copy in copies[3:6]:
        copy.wait()
    stream = emb[...].astype(F32) + dot_t(coef[...], basis[...])
    squares = jnp.sum(stream * stream, axis=-1, keepdims=True)

    def ready():
        for copy in copies[6:]:
            copy.wait()

    qkv_sums(stream, squares, gain[...], (w_q, w_kv), ready, out)


def project1_kernel(coef_a, coef_b, gain, basis, emb, w_q, w_kv, out):
    coef = coef_a[...] + coef_b[...]
    stream = emb[0, 1].astype(F32) + dot_t(coef, basis[...])
    squares = jnp.sum(stream * stream, axis=-1, keepdims=True)
    qkv_sums(stream, squares, gain[...], (w_q, w_kv), lambda: None, out)


def turn(value, cosine, sine):
    return value * cosine + pltpu.roll(value, HEAD // 2, 1) * sine


def finish_kernel(width, step, parts, tables, out):
    def total(at, rows):
        value = parts[0, at : at + rows, :].astype(F32)
        for source in range(1, PARTS):
            value += parts[source, at : at + rows, :].astype(F32)
        return value

    for at in range(QKV_ROWS, out.shape[1], 16):
        value = total(at, 16).astype(BF16)
        for to in range(PARTS):
            out[to, at : at + 16, :] = value
    cosine, sine = tables[2 * step], tables[2 * step + 1]
    tail = total(parts.shape[1] - TAIL, TAIL)
    squares = row_to_column(tail[0:1] + tail[1:2], OWN)
    inverse = lax.rsqrt(squares * (1.0 / width) + 1e-05)
    for head in range(WIDTH // HEAD):
        rows = slice(head * OWN, (head + 1) * OWN)
        value = total(head * OWN, OWN) * inverse
        if head <= GROUP:
            value = turn(value, cosine, sine)
        value = value.astype(BF16)
        for to in range(PARTS):
            out[to, rows, :] = value


def attention(gathered, lengths, attended):
    first = lengths[0]
    second = first + lengths[1]
    third = second + lengths[2]
    heads = [unpack(gathered, head * OWN, OWN) for head in range(WIDTH // HEAD)]
    for tile in range(ROWS // HEAD):
        at = tile * HEAD
        count = at + HEAD
        queries = jnp.concatenate([heads[h][at:count] for h in range(GROUP)], axis=0)
        keys = heads[GROUP][:count]
        values = jnp.concatenate([heads[GROUP + 1][:count], jnp.ones((count, HEAD), BF16)], axis=1)
        row = lax.broadcasted_iota(jnp.int32, (HEAD, count), 0) + at
        column = lax.broadcasted_iota(jnp.int32, (HEAD, count), 1)
        begin = jnp.where(row >= first, first, 0)
        begin = jnp.where(row >= second, second, begin)
        begin = jnp.where(row >= third, third, begin)
        allowed = (column >= begin) & (column <= row)
        scores = dot_t(queries, keys) * HEAD ** (-0.5)
        for h in range(GROUP):
            own = jnp.where(allowed, scores[h * HEAD : (h + 1) * HEAD], -1e30)
            weights = jnp.exp(own - jnp.max(own, axis=-1, keepdims=True)).astype(BF16)
            summed = dot(weights, values)
            attended[at:count, h * HEAD : (h + 1) * HEAD] = (
                summed[:, :HEAD] / summed[:, HEAD:]
            ).astype(BF16)


def boundary_panels(coef, attended, mixed):
    first, second = coef[:, :PANEL], coef[:, PANEL:]
    upper, cross, lower = symmetric_blocks(mixed)
    of_g = (dot(first, upper) + dot_t(second, cross), dot(first, cross) + dot(second, lower))
    columns = PANEL // HEAD
    return [
        (of_g[panel] + dot(attended[...], unpack(mixed, M_AT + panel * columns * M_OWN, M_OWN, columns))).astype(BF16)
        for panel in range(RANK // PANEL)
    ]


def first_kernel(parity, gathered, coef, lengths, out, attended):
    @pl.when(lax.axis_index("section") % 2 == parity)
    def _():
        attention(gathered, [lengths[0, 0, i] for i in range(3)], attended)
        for panel, value in enumerate(boundary_panels(coef, attended, gathered)):
            out[:, panel * PANEL : (panel + 1) * PANEL] = value


def second_kernel(
    gathered, mixed, coef_a, coef_b, before_odd, before_even, lengths, out, attended, buffer, sems
):
    odd = lax.axis_index("section") % 2 == 1

    @pl.when(odd)
    def _():
        buffer[0] = before_odd[...]

    @pl.when(jnp.logical_not(odd))
    def _():
        buffer[0] = before_even[...]

    copies = [pltpu.make_async_copy(buffer.at[0], out.at[0], sems.at[0])]
    copies[0].start()
    coef = coef_a[...] + coef_b[...]
    attention(gathered, [lengths[0, 1, i] for i in range(3)], attended)
    for panel, value in enumerate(boundary_panels(coef, attended, mixed)):
        columns = pl.ds(panel * PANEL, PANEL)
        buffer[1, :, columns] = value
        copies.append(
            pltpu.make_async_copy(
                buffer.at[1, :, columns], out.at[1, :, columns], sems.at[1 + panel]
            )
        )
        copies[-1].start()
    for copy in copies:
        copy.wait()


def exchange(blocks):
    return lax.all_to_all(blocks, "tensor", 0, 0)


def hop(value, parity):
    sections = lax.axis_size("section")
    pairs = [(s, s + 1) for s in range(sections - 1) if s % 2 == parity]
    return lax.ppermute(value, "section", pairs)


def local(state_coef, embed_terms, norm_gain, w_query, w_keyval, w_out, basis, doc_lengths):
    w_q, w_kv, w_o = w_query[0], w_keyval[0], w_out[0]
    depth = embed_terms.shape[-1]
    width = depth * PARTS
    shape = jax.ShapeDtypeStruct
    flops, moved = 2 * ROWS * depth * (RANK + WIDTH), 5 * MIB

    def finish(step, sent, tables, rows):
        return call(
            functools.partial(finish_kernel, width, step), f"finish{step}",
            shape((PARTS, rows, HEAD), BF16), [VMEM] * 2,
            16 * rows * HEAD, 3 * MIB, (exchange(sent), tables),
        )

    coef0 = state_coef[0]
    args = (doc_lengths, basis, w_o, coef0, embed_terms, norm_gain, w_q, w_kv)
    held = [pltpu.VMEM(arg.shape, BF16) for arg in args]
    held[0] = pltpu.SMEM(doc_lengths.shape, jnp.int32)
    held[4] = pltpu.VMEM((ROWS, depth), BF16)
    sent0, tables = call(
        project0_kernel, "project0",
        (pltpu.VMEM((PARTS, MIXED_ROWS + TAIL, HEAD), BF16), pltpu.VMEM((4, OWN, HEAD), F32)),
        [ANY] * len(args), 2 * flops, moved, args,
        held + [pltpu.SemaphoreType.DMA((len(args),))], (VMEM, VMEM), LIMIT0,
    )
    mixed = exchange(finish(0, sent0, tables, MIXED_ROWS))
    attended = pltpu.VMEM((ROWS, WIDTH_Q), BF16)
    attend_flops = 4 * ROWS * (ROWS * WIDTH_Q + RANK * RANK)
    step0 = (mixed, coef0, doc_lengths)
    boundary_even = call(
        functools.partial(first_kernel, 0), "attend0_even", shape((ROWS, RANK), BF16),
        [VMEM] * 2 + [SMEM], attend_flops, 3 * MIB, step0, [attended],
    )
    coef1_odd = hop(boundary_even, 0)
    boundary_odd = call(
        functools.partial(first_kernel, 1), "attend0_odd", shape((ROWS, RANK), BF16),
        [VMEM] * 2 + [SMEM], attend_flops, 3 * MIB, step0, [attended],
    )
    coef1 = (hop(boundary_odd, 1), coef1_odd)
    args = (*coef1, norm_gain, basis, embed_terms, w_q, w_kv)
    sent1 = call(
        project1_kernel, "project1", shape((PARTS, QKV_ROWS + TAIL, HEAD), BF16),
        [VMEM] * len(args), flops, moved, args,
    )
    heads = exchange(finish(1, sent1, tables, QKV_ROWS))
    both = call(
        second_kernel, "attend1", shape((2, ROWS, RANK), BF16), [VMEM] * 6 + [SMEM],
        attend_flops, 4 * MIB,
        (heads, mixed, *coef1, boundary_odd, boundary_even, doc_lengths),
        [attended, pltpu.VMEM((2, ROWS, RANK), BF16), pltpu.SemaphoreType.DMA((3,))], HBM,
    )
    return both[None]


def solution(mesh):
    return jax.shard_map(
        local,
        mesh=mesh,
        in_specs=(
            P("section", None, None),
            P("section", None, None, "tensor"),
            P("section", "tensor"),
            P("section", "tensor", None),
            P("section", "tensor", None),
            P("section", None, "tensor"),
            P("tensor", None),
            P("section", None, None),
        ),
        out_specs=P("section", None, None, None),
        check_vma=False,
    )
```

```python
import functools
import math

import jax
import jax.numpy as jnp
from jax import lax
from jax.experimental import pallas as pl
from jax.experimental.pallas import tpu as pltpu
from jax.sharding import PartitionSpec as P

HEAD = 128
GROUP = 4
WIDTH_Q = GROUP * HEAD
WIDTH = WIDTH_Q + 2 * HEAD
PARTS = 8
ROWS = 384
OWN = ROWS // PARTS
RANK = 512
PANEL = 256
M_OWN = RANK // PARTS
G_OWN = HEAD // PARTS
BF16 = jnp.bfloat16
F32 = jnp.float32
MIB = 1024 * 1024
LIMIT0 = 56

QKV_ROWS = OWN * (WIDTH // HEAD)
M_AT = QKV_ROWS
G_AT = M_AT + M_OWN * (RANK // HEAD)
G_BLOCKS = ((0, 0), (0, 1), (1, 1), (2, 2), (2, 3), (3, 3), (0, 2), (0, 3), (1, 2), (1, 3))
MIXED_ROWS = G_AT + len(G_BLOCKS) * G_OWN
TAIL = 16

VMEM = pl.BlockSpec(memory_space=pltpu.VMEM)
SMEM = pl.BlockSpec(memory_space=pltpu.SMEM)
ANY = pl.BlockSpec(memory_space=pl.ANY)
HBM = pl.BlockSpec(memory_space=pltpu.HBM)


def call(body, name, out_shape, in_specs, flops, moved, args, scratch=(), out_specs=VMEM, limit=16):
    return pl.pallas_call(
        body,
        name=name,
        out_shape=out_shape,
        in_specs=in_specs,
        out_specs=out_specs,
        scratch_shapes=scratch,
        cost_estimate=pl.CostEstimate(flops=flops, bytes_accessed=moved, transcendentals=0),
        compiler_params=pltpu.CompilerParams(vmem_limit_bytes=limit * MIB),
    )(*args)


def dot(a, b):
    return jnp.dot(a, b, preferred_element_type=F32)


def dot_t(a, b):
    return lax.dot_general(a, b, (((1,), (1,)), ((), ())), preferred_element_type=F32)


def column_to_row(column):
    shape = (column.shape[0], HEAD)
    row = lax.broadcasted_iota(jnp.int32, shape, 0)
    lane = lax.broadcasted_iota(jnp.int32, shape, 1)
    return jnp.sum(jnp.where(row == lane, column, 0.0), axis=0, keepdims=True)


def row_to_column(row_vector, rows):
    row = lax.broadcasted_iota(jnp.int32, (rows, HEAD), 0)
    lane = lax.broadcasted_iota(jnp.int32, (rows, HEAD), 1)
    return jnp.sum(jnp.where(row == lane, row_vector, 0.0), axis=1, keepdims=True)


def pack(out, value, at, rows):
    for column in range(value.shape[1] // HEAD):
        part = value[:, column * HEAD : (column + 1) * HEAD]
        for to in range(PARTS):
            out[to, at + column * rows : at + (column + 1) * rows, :] = part[
                to * rows : (to + 1) * rows
            ]


def unpack(packed, at, rows, columns=1):
    parts = [
        packed[:, at + column * rows : at + (column + 1) * rows, :].reshape(PARTS * rows, HEAD)
        for column in range(columns)
    ]
    return parts[0] if columns == 1 else jnp.concatenate(parts, axis=1)


def qkv_sums(stream, squares, gain, weights, ready, buffer):
    tail_at = buffer.shape[1] - TAIL
    scaled = (stream * gain.astype(F32)).astype(BF16)
    row = lax.broadcasted_iota(jnp.int32, (TAIL, HEAD), 0)
    for to in range(PARTS):
        laid = column_to_row(squares[to * OWN : (to + 1) * OWN])
        high = laid.astype(BF16).astype(F32)
        value = jnp.where(row == 0, high, jnp.where(row == 1, laid - high, 0.0))
        buffer[to, tail_at:, :] = value.astype(BF16)
    ready()
    w_q, w_kv = weights
    for panel in range(WIDTH // PANEL):
        if panel < WIDTH_Q // PANEL:
            weight = w_q[:, panel * PANEL : (panel + 1) * PANEL]
        else:
            weight = w_kv[...]
        pack(buffer, dot(scaled, weight).astype(BF16), panel * OWN * (PANEL // HEAD), OWN)


def rotary_tables(lengths, tables):
    lane = lax.broadcasted_iota(jnp.int32, (OWN, HEAD), 1)
    half = HEAD // 2
    pair = jnp.where(lane < half, lane, lane - half).astype(F32)
    frequency = jnp.exp(pair * (-math.log(500000.0) / half))
    index = lax.broadcasted_iota(jnp.int32, (OWN, HEAD), 0) + lax.axis_index("tensor") * OWN
    for step in range(2):
        end, begin = 0, jnp.zeros((OWN, HEAD), jnp.int32)
        for document in range(3):
            end = end + lengths[0, step, document]
            begin = jnp.where(index >= end, end, begin)
        angle = (index - begin).astype(F32) * frequency
        sine = jnp.sin(angle)
        tables[2 * step] = jnp.cos(angle)
        tables[2 * step + 1] = jnp.where(lane < half, -sine, sine)


def symmetric_sums(basis, buffer):
    left, right = basis[:, :PANEL], basis[:, PANEL:]
    turned = left.T
    parts = {
        (0, 0): dot(turned, left).astype(BF16),
        (0, 2): dot(turned, right).astype(BF16),
        (2, 2): dot(right.T, right).astype(BF16),
    }
    for place, (row, column) in enumerate(G_BLOCKS):
        part = parts[(row // 2 * 2, column // 2 * 2)]
        row, column = row % 2 * HEAD, column % 2 * HEAD
        block = part[row : row + HEAD, column : column + HEAD]
        pack(buffer, block, G_AT + place * G_OWN, G_OWN)


def symmetric_blocks(packed):
    blocks = {
        pair: unpack(packed, G_AT + place * G_OWN, G_OWN) for place, pair in enumerate(G_BLOCKS)
    }

    def part(row, column):
        corner = (
            blocks[(row + 1, column)] if row != column else blocks[(row, column + 1)].T
        )
        upper = jnp.concatenate([blocks[(row, column)], blocks[(row, column + 1)]], axis=1)
        lower = jnp.concatenate([corner, blocks[(row + 1, column + 1)]], axis=1)
        return jnp.concatenate([upper, lower], axis=0)

    return part(0, 0), part(0, 2), part(2, 2)


def project0_kernel(
    lengths_in, basis_in, wo_in, coef_in, emb_in, gain_in, wq_in, wkv_in, out, tables,
    lengths, basis, w_o, coef, emb, gain, w_q, w_kv, sems,
):
    pairs = [
        (lengths_in, lengths), (basis_in, basis), (wo_in, w_o), (coef_in, coef),
        (emb_in.at[0, 0], emb), (gain_in, gain), (wq_in, w_q), (wkv_in, w_kv),
    ]
    copies = [
        pltpu.make_async_copy(source, target, sems.at[i])
        for i, (source, target) in enumerate(pairs)
    ]
    for copy in copies[:3]:
        copy.start()
    copies[0].wait()
    for copy in copies[3:]:
        copy.start()
    rotary_tables(lengths, tables)
    copies[1].wait()
    copies[2].wait()
    pack(out, dot(w_o[...], basis[...]).astype(BF16), M_AT, M_OWN)
    symmetric_sums(basis, out)
    for copy in copies[3:6]:
        copy.wait()
    stream = emb[...].astype(F32) + dot_t(coef[...], basis[...])
    squares = jnp.sum(stream * stream, axis=-1, keepdims=True)

    def ready():
        for copy in copies[6:]:
            copy.wait()

    qkv_sums(stream, squares, gain[...], (w_q, w_kv), ready, out)


def project1_kernel(coef_a, coef_b, gain, basis, emb, w_q, w_kv, out):
    coef = coef_a[...] + coef_b[...]
    stream = emb[0, 1].astype(F32) + dot_t(coef, basis[...])
    squares = jnp.sum(stream * stream, axis=-1, keepdims=True)
    qkv_sums(stream, squares, gain[...], (w_q, w_kv), lambda: None, out)


def turn(value, cosine, sine):
    return value * cosine + pltpu.roll(value, HEAD // 2, 1) * sine


def finish_kernel(width, step, parts, tables, out):
    def total(at, rows):
        value = parts[0, at : at + rows, :].astype(F32)
        for source in range(1, PARTS):
            value += parts[source, at : at + rows, :].astype(F32)
        return value

    for at in range(QKV_ROWS, out.shape[1], 16):
        value = total(at, 16).astype(BF16)
        for to in range(PARTS):
            out[to, at : at + 16, :] = value
    cosine, sine = tables[2 * step], tables[2 * step + 1]
    tail = total(parts.shape[1] - TAIL, TAIL)
    squares = row_to_column(tail[0:1] + tail[1:2], OWN)
    inverse = lax.rsqrt(squares * (1.0 / width) + 1e-05)
    for head in range(WIDTH // HEAD):
        rows = slice(head * OWN, (head + 1) * OWN)
        value = total(head * OWN, OWN) * inverse
        if head <= GROUP:
            value = turn(value, cosine, sine)
        value = value.astype(BF16)
        for to in range(PARTS):
            out[to, rows, :] = value


def attention(gathered, lengths, attended):
    first = lengths[0]
    second = first + lengths[1]
    third = second + lengths[2]
    heads = [unpack(gathered, head * OWN, OWN) for head in range(WIDTH // HEAD)]
    for tile in range(ROWS // HEAD):
        at = tile * HEAD
        count = at + HEAD
        queries = jnp.concatenate([heads[h][at:count] for h in range(GROUP)], axis=0)
        keys = heads[GROUP][:count]
        values = jnp.concatenate([heads[GROUP + 1][:count], jnp.ones((count, HEAD), BF16)], axis=1)
        row = lax.broadcasted_iota(jnp.int32, (HEAD, count), 0) + at
        column = lax.broadcasted_iota(jnp.int32, (HEAD, count), 1)
        begin = jnp.where(row >= first, first, 0)
        begin = jnp.where(row >= second, second, begin)
        begin = jnp.where(row >= third, third, begin)
        allowed = (column >= begin) & (column <= row)
        scores = dot_t(queries, keys) * HEAD ** (-0.5)
        for h in range(GROUP):
            own = jnp.where(allowed, scores[h * HEAD : (h + 1) * HEAD], -1e30)
            weights = jnp.exp(own - jnp.max(own, axis=-1, keepdims=True)).astype(BF16)
            summed = dot(weights, values)
            attended[at:count, h * HEAD : (h + 1) * HEAD] = (
                summed[:, :HEAD] / summed[:, HEAD:]
            ).astype(BF16)


def boundary_panels(coef, attended, mixed):
    first, second = coef[:, :PANEL], coef[:, PANEL:]
    upper, cross, lower = symmetric_blocks(mixed)
    of_g = (dot(first, upper) + dot_t(second, cross), dot(first, cross) + dot(second, lower))
    columns = PANEL // HEAD
    return [
        (of_g[panel] + dot(attended[...], unpack(mixed, M_AT + panel * columns * M_OWN, M_OWN, columns))).astype(BF16)
        for panel in range(RANK // PANEL)
    ]


def first_kernel(parity, gathered, coef, lengths_in, out, attended, lengths, sem):
    @pl.when(lax.axis_index("section") % 2 == parity)
    def _():
        copy = pltpu.make_async_copy(lengths_in, lengths, sem)
        copy.start()
        copy.wait()
        attention(gathered, [lengths[0, 0, i] for i in range(3)], attended)
        for panel, value in enumerate(boundary_panels(coef, attended, gathered)):
            out[:, panel * PANEL : (panel + 1) * PANEL] = value


def second_kernel(
    gathered, mixed, coef_a, coef_b, before_odd, before_even, lengths_in, out,
    attended, buffer, lengths, sems,
):
    lengths_copy = pltpu.make_async_copy(lengths_in, lengths, sems.at[3])
    lengths_copy.start()
    odd = lax.axis_index("section") % 2 == 1
    from_odd = pltpu.make_async_copy(before_odd, out.at[0], sems.at[0])
    from_even = pltpu.make_async_copy(before_even, out.at[0], sems.at[4])
    pl.when(odd)(from_odd.start)
    pl.when(jnp.logical_not(odd))(from_even.start)
    copies = []
    lengths_copy.wait()
    coef = coef_a[...] + coef_b[...]
    attention(gathered, [lengths[0, 1, i] for i in range(3)], attended)
    for panel, value in enumerate(boundary_panels(coef, attended, mixed)):
        columns = pl.ds(panel * PANEL, PANEL)
        buffer[:, columns] = value
        copies.append(
            pltpu.make_async_copy(
                buffer.at[:, columns], out.at[1, :, columns], sems.at[1 + panel]
            )
        )
        copies[-1].start()
    for copy in copies:
        copy.wait()
    pl.when(odd)(from_odd.wait)
    pl.when(jnp.logical_not(odd))(from_even.wait)


def exchange(blocks):
    return lax.all_to_all(blocks, "tensor", 0, 0)


def hop(value, parity):
    sections = lax.axis_size("section")
    pairs = [(s, s + 1) for s in range(sections - 1) if s % 2 == parity]
    return lax.ppermute(value, "section", pairs)


def local(state_coef, embed_terms, norm_gain, w_query, w_keyval, w_out, basis, doc_lengths):
    w_q, w_kv, w_o = w_query[0], w_keyval[0], w_out[0]
    depth = embed_terms.shape[-1]
    width = depth * PARTS
    shape = jax.ShapeDtypeStruct
    flops, moved = 2 * ROWS * depth * (RANK + WIDTH), 5 * MIB

    def finish(step, sent, tables, rows):
        return call(
            functools.partial(finish_kernel, width, step), f"finish{step}",
            shape((PARTS, rows, HEAD), BF16), [VMEM] * 2,
            16 * rows * HEAD, 3 * MIB, (exchange(sent), tables),
        )

    coef0 = state_coef[0]
    args = (doc_lengths, basis, w_o, coef0, embed_terms, norm_gain, w_q, w_kv)
    held = [pltpu.VMEM(arg.shape, BF16) for arg in args]
    held[0] = pltpu.SMEM(doc_lengths.shape, jnp.int32)
    held[4] = pltpu.VMEM((ROWS, depth), BF16)
    sent0, tables = call(
        project0_kernel, "project0",
        (pltpu.VMEM((PARTS, MIXED_ROWS + TAIL, HEAD), BF16), pltpu.VMEM((4, OWN, HEAD), F32)),
        [ANY] * len(args), 2 * flops, moved, args,
        held + [pltpu.SemaphoreType.DMA((len(args),))], (VMEM, VMEM), LIMIT0,
    )
    mixed = exchange(finish(0, sent0, tables, MIXED_ROWS))
    attended = pltpu.VMEM((ROWS, WIDTH_Q), BF16)
    lengths = pltpu.SMEM(doc_lengths.shape, jnp.int32)
    attend_flops = 4 * ROWS * (ROWS * WIDTH_Q + RANK * RANK)
    step0 = (mixed, coef0, doc_lengths)
    boundary_even = call(
        functools.partial(first_kernel, 0), "attend0_even", shape((ROWS, RANK), BF16),
        [VMEM] * 2 + [ANY], attend_flops, 3 * MIB, step0,
        [attended, lengths, pltpu.SemaphoreType.DMA(())],
    )
    coef1_odd = hop(boundary_even, 0)
    boundary_odd = call(
        functools.partial(first_kernel, 1), "attend0_odd", shape((ROWS, RANK), BF16),
        [VMEM] * 2 + [ANY], attend_flops, 3 * MIB, step0,
        [attended, lengths, pltpu.SemaphoreType.DMA(())],
    )
    coef1 = (hop(boundary_odd, 1), coef1_odd)
    args = (*coef1, norm_gain, basis, embed_terms, w_q, w_kv)
    sent1 = call(
        project1_kernel, "project1", shape((PARTS, QKV_ROWS + TAIL, HEAD), BF16),
        [VMEM] * len(args), flops, moved, args,
    )
    heads = exchange(finish(1, sent1, tables, QKV_ROWS))
    both = call(
        second_kernel, "attend1", shape((2, ROWS, RANK), BF16), [VMEM] * 6 + [ANY],
        attend_flops, 4 * MIB,
        (heads, mixed, *coef1, boundary_odd, boundary_even, doc_lengths),
        [attended, pltpu.VMEM((ROWS, RANK), BF16), lengths, pltpu.SemaphoreType.DMA((5,))], HBM,
    )
    return both[None]


def solution(mesh):
    return jax.shard_map(
        local,
        mesh=mesh,
        in_specs=(
            P("section", None, None),
            P("section", None, None, "tensor"),
            P("section", "tensor"),
            P("section", "tensor", None),
            P("section", "tensor", None),
            P("section", None, "tensor"),
            P("tensor", None),
            P("section", None, None),
        ),
        out_specs=P("section", None, None, None),
        check_vma=False,
    )
```

```python
import functools
import math

import jax
import jax.numpy as jnp
from jax import lax
from jax.experimental import pallas as pl
from jax.experimental.pallas import tpu as pltpu
from jax.sharding import PartitionSpec as P

HEAD = 128
GROUP = 4
WIDTH_Q = GROUP * HEAD
WIDTH = WIDTH_Q + 2 * HEAD
PARTS = 8
ROWS = 384
OWN = ROWS // PARTS
RANK = 512
PANEL = 256
M_OWN = RANK // PARTS
G_OWN = HEAD // PARTS
BF16 = jnp.bfloat16
F32 = jnp.float32
MIB = 1024 * 1024
LIMIT0 = 56

QKV_ROWS = OWN * (WIDTH // HEAD)
M_AT = QKV_ROWS
G_AT = M_AT + M_OWN * (RANK // HEAD)
G_BLOCKS = ((0, 0), (0, 1), (1, 1), (2, 2), (2, 3), (3, 3), (0, 2), (0, 3), (1, 2), (1, 3))
MIXED_ROWS = G_AT + len(G_BLOCKS) * G_OWN
TAIL = 16

VMEM = pl.BlockSpec(memory_space=pltpu.VMEM)
SMEM = pl.BlockSpec(memory_space=pltpu.SMEM)
ANY = pl.BlockSpec(memory_space=pl.ANY)
HBM = pl.BlockSpec(memory_space=pltpu.HBM)


def call(body, name, out_shape, in_specs, flops, moved, args, scratch=(), out_specs=VMEM, limit=16):
    return pl.pallas_call(
        body,
        name=name,
        out_shape=out_shape,
        in_specs=in_specs,
        out_specs=out_specs,
        scratch_shapes=scratch,
        cost_estimate=pl.CostEstimate(flops=flops, bytes_accessed=moved, transcendentals=0),
        compiler_params=pltpu.CompilerParams(vmem_limit_bytes=limit * MIB),
    )(*args)


def dot(a, b):
    return jnp.dot(a, b, preferred_element_type=F32)


def dot_t(a, b):
    return lax.dot_general(a, b, (((1,), (1,)), ((), ())), preferred_element_type=F32)


def column_to_row(column):
    shape = (column.shape[0], HEAD)
    row = lax.broadcasted_iota(jnp.int32, shape, 0)
    lane = lax.broadcasted_iota(jnp.int32, shape, 1)
    return jnp.sum(jnp.where(row == lane, column, 0.0), axis=0, keepdims=True)


def row_to_column(row_vector, rows):
    row = lax.broadcasted_iota(jnp.int32, (rows, HEAD), 0)
    lane = lax.broadcasted_iota(jnp.int32, (rows, HEAD), 1)
    return jnp.sum(jnp.where(row == lane, row_vector, 0.0), axis=1, keepdims=True)


def pack(out, value, at, rows):
    for column in range(value.shape[1] // HEAD):
        part = value[:, column * HEAD : (column + 1) * HEAD]
        for to in range(PARTS):
            out[to, at + column * rows : at + (column + 1) * rows, :] = part[
                to * rows : (to + 1) * rows
            ]


def unpack(packed, at, rows, columns=1):
    parts = [
        packed[:, at + column * rows : at + (column + 1) * rows, :].reshape(PARTS * rows, HEAD)
        for column in range(columns)
    ]
    return parts[0] if columns == 1 else jnp.concatenate(parts, axis=1)


def qkv_sums(stream, squares, gain, weights, ready, buffer):
    tail_at = buffer.shape[1] - TAIL
    scaled = (stream * gain.astype(F32)).astype(BF16)
    row = lax.broadcasted_iota(jnp.int32, (TAIL, HEAD), 0)
    for to in range(PARTS):
        laid = column_to_row(squares[to * OWN : (to + 1) * OWN])
        high = laid.astype(BF16).astype(F32)
        value = jnp.where(row == 0, high, jnp.where(row == 1, laid - high, 0.0))
        buffer[to, tail_at:, :] = value.astype(BF16)
    ready()
    w_q, w_kv = weights
    for panel in range(WIDTH // PANEL):
        if panel < WIDTH_Q // PANEL:
            weight = w_q[:, panel * PANEL : (panel + 1) * PANEL]
        else:
            weight = w_kv[...]
        pack(buffer, dot(scaled, weight).astype(BF16), panel * OWN * (PANEL // HEAD), OWN)


def rotary_tables(lengths, tables):
    lane = lax.broadcasted_iota(jnp.int32, (OWN, HEAD), 1)
    half = HEAD // 2
    pair = jnp.where(lane < half, lane, lane - half).astype(F32)
    frequency = jnp.exp(pair * (-math.log(500000.0) / half))
    index = lax.broadcasted_iota(jnp.int32, (OWN, HEAD), 0) + lax.axis_index("tensor") * OWN
    for step in range(2):
        end, begin = 0, jnp.zeros((OWN, HEAD), jnp.int32)
        for document in range(3):
            end = end + lengths[0, step, document]
            begin = jnp.where(index >= end, end, begin)
        angle = (index - begin).astype(F32) * frequency
        sine = jnp.sin(angle)
        tables[2 * step] = jnp.cos(angle)
        tables[2 * step + 1] = jnp.where(lane < half, -sine, sine)


def symmetric_sums(basis, buffer):
    left, right = basis[:, :PANEL], basis[:, PANEL:]
    turned = left.T
    parts = {
        (0, 0): dot(turned, left).astype(BF16),
        (0, 2): dot(turned, right).astype(BF16),
        (2, 2): dot(right.T, right).astype(BF16),
    }
    for place, (row, column) in enumerate(G_BLOCKS):
        part = parts[(row // 2 * 2, column // 2 * 2)]
        row, column = row % 2 * HEAD, column % 2 * HEAD
        block = part[row : row + HEAD, column : column + HEAD]
        pack(buffer, block, G_AT + place * G_OWN, G_OWN)


def symmetric_blocks(packed):
    blocks = {
        pair: unpack(packed, G_AT + place * G_OWN, G_OWN) for place, pair in enumerate(G_BLOCKS)
    }

    def part(row, column):
        corner = (
            blocks[(row + 1, column)] if row != column else blocks[(row, column + 1)].T
        )
        upper = jnp.concatenate([blocks[(row, column)], blocks[(row, column + 1)]], axis=1)
        lower = jnp.concatenate([corner, blocks[(row + 1, column + 1)]], axis=1)
        return jnp.concatenate([upper, lower], axis=0)

    return part(0, 0), part(0, 2), part(2, 2)


def project0_kernel(
    lengths_in, basis_in, wo_in, coef_in, emb_in, gain_in, wq_in, wkv_in, out, tables,
    lengths, basis, w_o, coef, emb, gain, w_q, w_kv, sems,
):
    pairs = [
        (lengths_in, lengths), (basis_in, basis), (wo_in, w_o), (coef_in, coef),
        (emb_in.at[0, 0], emb), (gain_in, gain), (wq_in, w_q), (wkv_in, w_kv),
    ]
    copies = [
        pltpu.make_async_copy(source, target, sems.at[i])
        for i, (source, target) in enumerate(pairs)
    ]
    for copy in copies[:3]:
        copy.start()
    copies[0].wait()
    for copy in copies[3:]:
        copy.start()
    rotary_tables(lengths, tables)
    copies[1].wait()
    copies[2].wait()
    pack(out, dot(w_o[...], basis[...]).astype(BF16), M_AT, M_OWN)
    symmetric_sums(basis, out)
    for copy in copies[3:6]:
        copy.wait()
    stream = emb[...].astype(F32) + dot_t(coef[...], basis[...])
    squares = jnp.sum(stream * stream, axis=-1, keepdims=True)

    def ready():
        for copy in copies[6:]:
            copy.wait()

    qkv_sums(stream, squares, gain[...], (w_q, w_kv), ready, out)


def project1_kernel(coef_a, coef_b, gain, basis, emb, w_q, w_kv, out):
    coef = coef_a[...] + coef_b[...]
    stream = emb[0, 1].astype(F32) + dot_t(coef, basis[...])
    squares = jnp.sum(stream * stream, axis=-1, keepdims=True)
    qkv_sums(stream, squares, gain[...], (w_q, w_kv), lambda: None, out)


def turn(value, cosine, sine):
    return value * cosine + pltpu.roll(value, HEAD // 2, 1) * sine


def finish_kernel(width, step, parts, tables, out):
    def total(at, rows):
        value = parts[0, at : at + rows, :].astype(F32)
        for source in range(1, PARTS):
            value += parts[source, at : at + rows, :].astype(F32)
        return value

    for at in range(QKV_ROWS, out.shape[1], 16):
        value = total(at, 16).astype(BF16)
        for to in range(PARTS):
            out[to, at : at + 16, :] = value
    cosine, sine = tables[2 * step], tables[2 * step + 1]
    tail = total(parts.shape[1] - TAIL, TAIL)
    squares = row_to_column(tail[0:1] + tail[1:2], OWN)
    inverse = lax.rsqrt(squares * (1.0 / width) + 1e-05)
    for head in range(WIDTH // HEAD):
        rows = slice(head * OWN, (head + 1) * OWN)
        value = total(head * OWN, OWN) * inverse
        if head <= GROUP:
            value = turn(value, cosine, sine)
        value = value.astype(BF16)
        for to in range(PARTS):
            out[to, rows, :] = value


def attention(gathered, lengths, attended):
    first = lengths[0]
    second = first + lengths[1]
    third = second + lengths[2]
    heads = [unpack(gathered, head * OWN, OWN) for head in range(WIDTH // HEAD)]
    for tile in range(ROWS // HEAD):
        at = tile * HEAD
        count = at + HEAD
        queries = jnp.concatenate([heads[h][at:count] for h in range(GROUP)], axis=0)
        keys = heads[GROUP][:count]
        values = jnp.concatenate([heads[GROUP + 1][:count], jnp.ones((count, HEAD), BF16)], axis=1)
        row = lax.broadcasted_iota(jnp.int32, (HEAD, count), 0) + at
        column = lax.broadcasted_iota(jnp.int32, (HEAD, count), 1)
        begin = jnp.where(row >= first, first, 0)
        begin = jnp.where(row >= second, second, begin)
        begin = jnp.where(row >= third, third, begin)
        bias = jnp.where((column >= begin) & (column <= row), 0.0, -1e30)
        scores = dot_t(queries, keys).reshape(GROUP, HEAD, count) * HEAD ** (-0.5) + bias[None]
        scores = scores.reshape(GROUP * HEAD, count)
        weights = jnp.exp(scores - jnp.max(scores, axis=-1, keepdims=True)).astype(BF16)
        summed = dot(weights, values)
        result = (summed[:, :HEAD] / summed[:, HEAD:]).astype(BF16)
        for h in range(GROUP):
            attended[at:count, h * HEAD : (h + 1) * HEAD] = result[h * HEAD : (h + 1) * HEAD]


def boundary_panels(coef, attended, mixed):
    first, second = coef[:, :PANEL], coef[:, PANEL:]
    upper, cross, lower = symmetric_blocks(mixed)
    of_g = (dot(first, upper) + dot_t(second, cross), dot(first, cross) + dot(second, lower))
    columns = PANEL // HEAD
    return [
        (of_g[panel] + dot(attended[...], unpack(mixed, M_AT + panel * columns * M_OWN, M_OWN, columns))).astype(BF16)
        for panel in range(RANK // PANEL)
    ]


def first_kernel(parity, gathered, coef, lengths_in, out, attended, lengths, sem):
    @pl.when(lax.axis_index("section") % 2 == parity)
    def _():
        copy = pltpu.make_async_copy(lengths_in, lengths, sem)
        copy.start()
        copy.wait()
        attention(gathered, [lengths[0, 0, i] for i in range(3)], attended)
        for panel, value in enumerate(boundary_panels(coef, attended, gathered)):
            out[:, panel * PANEL : (panel + 1) * PANEL] = value


def second_kernel(
    gathered, mixed, coef_a, coef_b, before_odd, before_even, lengths_in, out,
    attended, buffer, lengths, sems,
):
    lengths_copy = pltpu.make_async_copy(lengths_in, lengths, sems.at[3])
    lengths_copy.start()
    odd = lax.axis_index("section") % 2 == 1
    from_odd = pltpu.make_async_copy(before_odd, out.at[0], sems.at[0])
    from_even = pltpu.make_async_copy(before_even, out.at[0], sems.at[4])
    pl.when(odd)(from_odd.start)
    pl.when(jnp.logical_not(odd))(from_even.start)
    copies = []
    lengths_copy.wait()
    coef = coef_a[...] + coef_b[...]
    attention(gathered, [lengths[0, 1, i] for i in range(3)], attended)
    for panel, value in enumerate(boundary_panels(coef, attended, mixed)):
        columns = pl.ds(panel * PANEL, PANEL)
        buffer[:, columns] = value
        copies.append(
            pltpu.make_async_copy(
                buffer.at[:, columns], out.at[1, :, columns], sems.at[1 + panel]
            )
        )
        copies[-1].start()
    for copy in copies:
        copy.wait()
    pl.when(odd)(from_odd.wait)
    pl.when(jnp.logical_not(odd))(from_even.wait)


def exchange(blocks):
    return lax.all_to_all(blocks, "tensor", 0, 0)


def hop(value, parity):
    sections = lax.axis_size("section")
    pairs = [(s, s + 1) for s in range(sections - 1) if s % 2 == parity]
    return lax.ppermute(value, "section", pairs)


def local(state_coef, embed_terms, norm_gain, w_query, w_keyval, w_out, basis, doc_lengths):
    w_q, w_kv, w_o = w_query[0], w_keyval[0], w_out[0]
    depth = embed_terms.shape[-1]
    width = depth * PARTS
    shape = jax.ShapeDtypeStruct
    flops, moved = 2 * ROWS * depth * (RANK + WIDTH), 5 * MIB

    def finish(step, sent, tables, rows):
        return call(
            functools.partial(finish_kernel, width, step), f"finish{step}",
            shape((PARTS, rows, HEAD), BF16), [VMEM] * 2,
            16 * rows * HEAD, 3 * MIB, (exchange(sent), tables),
        )

    coef0 = state_coef[0]
    args = (doc_lengths, basis, w_o, coef0, embed_terms, norm_gain, w_q, w_kv)
    held = [pltpu.VMEM(arg.shape, BF16) for arg in args]
    held[0] = pltpu.SMEM(doc_lengths.shape, jnp.int32)
    held[4] = pltpu.VMEM((ROWS, depth), BF16)
    sent0, tables = call(
        project0_kernel, "project0",
        (pltpu.VMEM((PARTS, MIXED_ROWS + TAIL, HEAD), BF16), pltpu.VMEM((4, OWN, HEAD), F32)),
        [ANY] * len(args), 2 * flops, moved, args,
        held + [pltpu.SemaphoreType.DMA((len(args),))], (VMEM, VMEM), LIMIT0,
    )
    mixed = exchange(finish(0, sent0, tables, MIXED_ROWS))
    attended = pltpu.VMEM((ROWS, WIDTH_Q), BF16)
    lengths = pltpu.SMEM(doc_lengths.shape, jnp.int32)
    attend_flops = 4 * ROWS * (ROWS * WIDTH_Q + RANK * RANK)
    step0 = (mixed, coef0, doc_lengths)
    boundary_even = call(
        functools.partial(first_kernel, 0), "attend0_even", shape((ROWS, RANK), BF16),
        [VMEM] * 2 + [ANY], attend_flops, 3 * MIB, step0,
        [attended, lengths, pltpu.SemaphoreType.DMA(())],
    )
    coef1_odd = hop(boundary_even, 0)
    boundary_odd = call(
        functools.partial(first_kernel, 1), "attend0_odd", shape((ROWS, RANK), BF16),
        [VMEM] * 2 + [ANY], attend_flops, 3 * MIB, step0,
        [attended, lengths, pltpu.SemaphoreType.DMA(())],
    )
    coef1 = (hop(boundary_odd, 1), coef1_odd)
    args = (*coef1, norm_gain, basis, embed_terms, w_q, w_kv)
    sent1 = call(
        project1_kernel, "project1", shape((PARTS, QKV_ROWS + TAIL, HEAD), BF16),
        [VMEM] * len(args), flops, moved, args,
    )
    heads = exchange(finish(1, sent1, tables, QKV_ROWS))
    both = call(
        second_kernel, "attend1", shape((2, ROWS, RANK), BF16), [VMEM] * 6 + [ANY],
        attend_flops, 4 * MIB,
        (heads, mixed, *coef1, boundary_odd, boundary_even, doc_lengths),
        [attended, pltpu.VMEM((ROWS, RANK), BF16), lengths, pltpu.SemaphoreType.DMA((5,))], HBM,
    )
    return both[None]


def solution(mesh):
    return jax.shard_map(
        local,
        mesh=mesh,
        in_specs=(
            P("section", None, None),
            P("section", None, None, "tensor"),
            P("section", "tensor"),
            P("section", "tensor", None),
            P("section", "tensor", None),
            P("section", None, "tensor"),
            P("tensor", None),
            P("section", None, None),
        ),
        out_specs=P("section", None, None, None),
        check_vma=False,
    )
```

```python
import functools
import math

import jax
import jax.numpy as jnp
from jax import lax
from jax.experimental import pallas as pl
from jax.experimental.pallas import tpu as pltpu
from jax.sharding import PartitionSpec as P

HEAD = 128
GROUP = 4
WIDTH_Q = GROUP * HEAD
WIDTH = WIDTH_Q + 2 * HEAD
PARTS = 8
ROWS = 384
OWN = ROWS // PARTS
RANK = 512
PANEL = 256
M_OWN = RANK // PARTS
G_OWN = HEAD // PARTS
BF16 = jnp.bfloat16
F32 = jnp.float32
MIB = 1024 * 1024
LIMIT0 = 56

QKV_ROWS = OWN * (WIDTH // HEAD)
M_AT = QKV_ROWS
G_AT = M_AT + M_OWN * (RANK // HEAD)
G_BLOCKS = ((0, 0), (0, 1), (1, 1), (2, 2), (2, 3), (3, 3), (0, 2), (0, 3), (1, 2), (1, 3))
MIXED_ROWS = G_AT + len(G_BLOCKS) * G_OWN
TAIL = 16

VMEM = pl.BlockSpec(memory_space=pltpu.VMEM)
SMEM = pl.BlockSpec(memory_space=pltpu.SMEM)
ANY = pl.BlockSpec(memory_space=pl.ANY)
HBM = pl.BlockSpec(memory_space=pltpu.HBM)


def call(body, name, out_shape, in_specs, flops, moved, args, scratch=(), out_specs=VMEM, limit=16):
    return pl.pallas_call(
        body,
        name=name,
        out_shape=out_shape,
        in_specs=in_specs,
        out_specs=out_specs,
        scratch_shapes=scratch,
        cost_estimate=pl.CostEstimate(flops=flops, bytes_accessed=moved, transcendentals=0),
        compiler_params=pltpu.CompilerParams(vmem_limit_bytes=limit * MIB),
    )(*args)


def dot(a, b):
    return jnp.dot(a, b, preferred_element_type=F32)


def dot_t(a, b):
    return lax.dot_general(a, b, (((1,), (1,)), ((), ())), preferred_element_type=F32)


def column_to_row(column):
    shape = (column.shape[0], HEAD)
    row = lax.broadcasted_iota(jnp.int32, shape, 0)
    lane = lax.broadcasted_iota(jnp.int32, shape, 1)
    return jnp.sum(jnp.where(row == lane, column, 0.0), axis=0, keepdims=True)


def row_to_column(row_vector, rows):
    row = lax.broadcasted_iota(jnp.int32, (rows, HEAD), 0)
    lane = lax.broadcasted_iota(jnp.int32, (rows, HEAD), 1)
    return jnp.sum(jnp.where(row == lane, row_vector, 0.0), axis=1, keepdims=True)


def pack(out, value, at, rows):
    for column in range(value.shape[1] // HEAD):
        part = value[:, column * HEAD : (column + 1) * HEAD]
        for to in range(PARTS):
            out[to, at + column * rows : at + (column + 1) * rows, :] = part[
                to * rows : (to + 1) * rows
            ]


def unpack(packed, at, rows, columns=1):
    parts = [
        packed[:, at + column * rows : at + (column + 1) * rows, :].reshape(PARTS * rows, HEAD)
        for column in range(columns)
    ]
    return parts[0] if columns == 1 else jnp.concatenate(parts, axis=1)


def qkv_sums(stream, squares, gain, weights, ready, buffer):
    tail_at = buffer.shape[1] - TAIL
    scaled = (stream * gain.astype(F32)).astype(BF16)
    row = lax.broadcasted_iota(jnp.int32, (TAIL, HEAD), 0)
    for to in range(PARTS):
        laid = column_to_row(squares[to * OWN : (to + 1) * OWN])
        high = laid.astype(BF16).astype(F32)
        value = jnp.where(row == 0, high, jnp.where(row == 1, laid - high, 0.0))
        buffer[to, tail_at:, :] = value.astype(BF16)
    ready()
    w_q, w_kv = weights
    for panel in range(WIDTH // PANEL):
        if panel < WIDTH_Q // PANEL:
            weight = w_q[:, panel * PANEL : (panel + 1) * PANEL]
        else:
            weight = w_kv[...]
        pack(buffer, dot(scaled, weight).astype(BF16), panel * OWN * (PANEL // HEAD), OWN)


def rotary_tables(lengths, tables):
    lane = lax.broadcasted_iota(jnp.int32, (OWN, HEAD), 1)
    half = HEAD // 2
    pair = jnp.where(lane < half, lane, lane - half).astype(F32)
    frequency = jnp.exp(pair * (-math.log(500000.0) / half))
    index = lax.broadcasted_iota(jnp.int32, (OWN, HEAD), 0) + lax.axis_index("tensor") * OWN
    for step in range(2):
        end, begin = 0, jnp.zeros((OWN, HEAD), jnp.int32)
        for document in range(3):
            end = end + lengths[0, step, document]
            begin = jnp.where(index >= end, end, begin)
        angle = (index - begin).astype(F32) * frequency
        sine = jnp.sin(angle)
        tables[2 * step] = jnp.cos(angle)
        tables[2 * step + 1] = jnp.where(lane < half, -sine, sine)


def symmetric_sums(basis, buffer):
    left, right = basis[:, :PANEL], basis[:, PANEL:]
    turned = left.T
    parts = {
        (0, 0): dot(turned, left).astype(BF16),
        (0, 2): dot(turned, right).astype(BF16),
        (2, 2): dot(right.T, right).astype(BF16),
    }
    for place, (row, column) in enumerate(G_BLOCKS):
        part = parts[(row // 2 * 2, column // 2 * 2)]
        row, column = row % 2 * HEAD, column % 2 * HEAD
        block = part[row : row + HEAD, column : column + HEAD]
        pack(buffer, block, G_AT + place * G_OWN, G_OWN)


def symmetric_blocks(packed):
    blocks = {
        pair: unpack(packed, G_AT + place * G_OWN, G_OWN) for place, pair in enumerate(G_BLOCKS)
    }

    def part(row, column):
        corner = (
            blocks[(row + 1, column)] if row != column else blocks[(row, column + 1)].T
        )
        upper = jnp.concatenate([blocks[(row, column)], blocks[(row, column + 1)]], axis=1)
        lower = jnp.concatenate([corner, blocks[(row + 1, column + 1)]], axis=1)
        return jnp.concatenate([upper, lower], axis=0)

    return part(0, 0), part(0, 2), part(2, 2)


def project0_kernel(
    lengths_in, basis_in, wo_in, coef_in, emb_in, gain_in, wq_in, wkv_in, out, tables,
    lengths, basis, w_o, coef, emb, gain, w_q, w_kv, sems,
):
    pairs = [
        (lengths_in, lengths), (basis_in, basis), (wo_in, w_o), (coef_in, coef),
        (emb_in.at[0, 0], emb), (gain_in, gain), (wq_in, w_q), (wkv_in, w_kv),
    ]
    copies = [
        pltpu.make_async_copy(source, target, sems.at[i])
        for i, (source, target) in enumerate(pairs)
    ]
    for copy in copies[:3]:
        copy.start()
    copies[0].wait()
    for copy in copies[3:]:
        copy.start()
    rotary_tables(lengths, tables)
    copies[1].wait()
    copies[2].wait()
    pack(out, dot(w_o[...], basis[...]).astype(BF16), M_AT, M_OWN)
    symmetric_sums(basis, out)
    for copy in copies[3:6]:
        copy.wait()
    stream = emb[...].astype(F32) + dot_t(coef[...], basis[...])
    squares = jnp.sum(stream * stream, axis=-1, keepdims=True)

    def ready():
        for copy in copies[6:]:
            copy.wait()

    qkv_sums(stream, squares, gain[...], (w_q, w_kv), ready, out)


def project1_kernel(coef_a, coef_b, gain, basis, emb, w_q, w_kv, out):
    coef = coef_a[...] + coef_b[...]
    stream = emb[0, 1].astype(F32) + dot_t(coef, basis[...])
    squares = jnp.sum(stream * stream, axis=-1, keepdims=True)
    qkv_sums(stream, squares, gain[...], (w_q, w_kv), lambda: None, out)


def turn(value, cosine, sine):
    return value * cosine + pltpu.roll(value, HEAD // 2, 1) * sine


def finish_kernel(width, step, parts, tables, out):
    def total(at, rows):
        value = parts[0, at : at + rows, :].astype(F32)
        for source in range(1, PARTS):
            value += parts[source, at : at + rows, :].astype(F32)
        return value

    for at in range(QKV_ROWS, out.shape[1], 16):
        value = total(at, 16).astype(BF16)
        for to in range(PARTS):
            out[to, at : at + 16, :] = value
    cosine, sine = tables[2 * step], tables[2 * step + 1]
    tail = total(parts.shape[1] - TAIL, TAIL)
    squares = row_to_column(tail[0:1] + tail[1:2], OWN)
    inverse = lax.rsqrt(squares * (1.0 / width) + 1e-05)
    for head in range(WIDTH // HEAD):
        rows = slice(head * OWN, (head + 1) * OWN)
        value = total(head * OWN, OWN) * inverse
        if head <= GROUP:
            value = turn(value, cosine, sine)
        value = value.astype(BF16)
        for to in range(PARTS):
            out[to, rows, :] = value


def attention(gathered, lengths, attended):
    first = lengths[0]
    second = first + lengths[1]
    third = second + lengths[2]
    heads = [unpack(gathered, head * OWN, OWN) for head in range(WIDTH // HEAD)]
    for tile in range(ROWS // HEAD):
        at = tile * HEAD
        count = at + HEAD
        queries = jnp.concatenate([heads[h][at:count] for h in range(GROUP)], axis=0)
        keys = heads[GROUP][:count]
        values = jnp.concatenate([heads[GROUP + 1][:count], jnp.ones((count, HEAD), BF16)], axis=1)
        row = lax.broadcasted_iota(jnp.int32, (HEAD, count), 0) + at
        column = lax.broadcasted_iota(jnp.int32, (HEAD, count), 1)
        begin = jnp.where(row >= first, first, 0)
        begin = jnp.where(row >= second, second, begin)
        begin = jnp.where(row >= third, third, begin)
        allowed = (column >= begin) & (column <= row)
        scores = dot_t(queries, keys) * HEAD ** (-0.5)
        for h in range(GROUP):
            own = jnp.where(allowed, scores[h * HEAD : (h + 1) * HEAD], -1e30)
            weights = jnp.exp(own - jnp.max(own, axis=-1, keepdims=True)).astype(BF16)
            summed = dot(weights, values)
            attended[at:count, h * HEAD : (h + 1) * HEAD] = (
                summed[:, :HEAD] / summed[:, HEAD:]
            ).astype(BF16)


def carried_panels(coef, mixed):
    first, second = coef[:, :PANEL], coef[:, PANEL:]
    upper, cross, lower = symmetric_blocks(mixed)
    return dot(first, upper) + dot_t(second, cross), dot(first, cross) + dot(second, lower)


def boundary_panels(carried, attended, mixed):
    columns = PANEL // HEAD
    return [
        (
            carried[panel]
            + dot(attended[...], unpack(mixed, M_AT + panel * columns * M_OWN, M_OWN, columns))
        ).astype(BF16)
        for panel in range(RANK // PANEL)
    ]


def first_kernel(parity, gathered, coef, lengths_in, out, attended, lengths, sem):
    @pl.when(lax.axis_index("section") % 2 == parity)
    def _():
        copy = pltpu.make_async_copy(lengths_in, lengths, sem)
        copy.start()
        carried = carried_panels(coef[...], gathered)
        copy.wait()
        attention(gathered, [lengths[0, 0, i] for i in range(3)], attended)
        for panel, value in enumerate(boundary_panels(carried, attended, gathered)):
            out[:, panel * PANEL : (panel + 1) * PANEL] = value


def second_kernel(
    gathered, mixed, coef_a, coef_b, before_odd, before_even, lengths_in, out,
    attended, buffer, lengths, sems,
):
    lengths_copy = pltpu.make_async_copy(lengths_in, lengths, sems.at[3])
    lengths_copy.start()
    odd = lax.axis_index("section") % 2 == 1
    from_odd = pltpu.make_async_copy(before_odd, out.at[0], sems.at[0])
    from_even = pltpu.make_async_copy(before_even, out.at[0], sems.at[4])
    pl.when(odd)(from_odd.start)
    pl.when(jnp.logical_not(odd))(from_even.start)
    copies = []
    carried = carried_panels(coef_a[...] + coef_b[...], mixed)
    lengths_copy.wait()
    attention(gathered, [lengths[0, 1, i] for i in range(3)], attended)
    for panel, value in enumerate(boundary_panels(carried, attended, mixed)):
        columns = pl.ds(panel * PANEL, PANEL)
        buffer[:, columns] = value
        copies.append(
            pltpu.make_async_copy(
                buffer.at[:, columns], out.at[1, :, columns], sems.at[1 + panel]
            )
        )
        copies[-1].start()
    for copy in copies:
        copy.wait()
    pl.when(odd)(from_odd.wait)
    pl.when(jnp.logical_not(odd))(from_even.wait)


def exchange(blocks):
    return lax.all_to_all(blocks, "tensor", 0, 0)


def hop(value, parity):
    sections = lax.axis_size("section")
    pairs = [(s, s + 1) for s in range(sections - 1) if s % 2 == parity]
    return lax.ppermute(value, "section", pairs)


def local(state_coef, embed_terms, norm_gain, w_query, w_keyval, w_out, basis, doc_lengths):
    w_q, w_kv, w_o = w_query[0], w_keyval[0], w_out[0]
    depth = embed_terms.shape[-1]
    width = depth * PARTS
    shape = jax.ShapeDtypeStruct
    flops, moved = 2 * ROWS * depth * (RANK + WIDTH), 5 * MIB

    def finish(step, sent, tables, rows):
        return call(
            functools.partial(finish_kernel, width, step), f"finish{step}",
            shape((PARTS, rows, HEAD), BF16), [VMEM] * 2,
            16 * rows * HEAD, 3 * MIB, (exchange(sent), tables),
        )

    coef0 = state_coef[0]
    args = (doc_lengths, basis, w_o, coef0, embed_terms, norm_gain, w_q, w_kv)
    held = [pltpu.VMEM(arg.shape, BF16) for arg in args]
    held[0] = pltpu.SMEM(doc_lengths.shape, jnp.int32)
    held[4] = pltpu.VMEM((ROWS, depth), BF16)
    sent0, tables = call(
        project0_kernel, "project0",
        (pltpu.VMEM((PARTS, MIXED_ROWS + TAIL, HEAD), BF16), pltpu.VMEM((4, OWN, HEAD), F32)),
        [ANY] * len(args), 2 * flops, moved, args,
        held + [pltpu.SemaphoreType.DMA((len(args),))], (VMEM, VMEM), LIMIT0,
    )
    mixed = exchange(finish(0, sent0, tables, MIXED_ROWS))
    attended = pltpu.VMEM((ROWS, WIDTH_Q), BF16)
    lengths = pltpu.SMEM(doc_lengths.shape, jnp.int32)
    attend_flops = 4 * ROWS * (ROWS * WIDTH_Q + RANK * RANK)
    step0 = (mixed, coef0, doc_lengths)
    boundary_even = call(
        functools.partial(first_kernel, 0), "attend0_even", shape((ROWS, RANK), BF16),
        [VMEM] * 2 + [ANY], attend_flops, 3 * MIB, step0,
        [attended, lengths, pltpu.SemaphoreType.DMA(())],
    )
    coef1_odd = hop(boundary_even, 0)
    boundary_odd = call(
        functools.partial(first_kernel, 1), "attend0_odd", shape((ROWS, RANK), BF16),
        [VMEM] * 2 + [ANY], attend_flops, 3 * MIB, step0,
        [attended, lengths, pltpu.SemaphoreType.DMA(())],
    )
    coef1 = (hop(boundary_odd, 1), coef1_odd)
    args = (*coef1, norm_gain, basis, embed_terms, w_q, w_kv)
    sent1 = call(
        project1_kernel, "project1", shape((PARTS, QKV_ROWS + TAIL, HEAD), BF16),
        [VMEM] * len(args), flops, moved, args,
    )
    heads = exchange(finish(1, sent1, tables, QKV_ROWS))
    both = call(
        second_kernel, "attend1", shape((2, ROWS, RANK), BF16), [VMEM] * 6 + [ANY],
        attend_flops, 4 * MIB,
        (heads, mixed, *coef1, boundary_odd, boundary_even, doc_lengths),
        [attended, pltpu.VMEM((ROWS, RANK), BF16), lengths, pltpu.SemaphoreType.DMA((5,))], HBM,
    )
    return both[None]


def solution(mesh):
    return jax.shard_map(
        local,
        mesh=mesh,
        in_specs=(
            P("section", None, None),
            P("section", None, None, "tensor"),
            P("section", "tensor"),
            P("section", "tensor", None),
            P("section", "tensor", None),
            P("section", None, "tensor"),
            P("tensor", None),
            P("section", None, None),
        ),
        out_specs=P("section", None, None, None),
        check_vma=False,
    )
```

```python
import functools
import math

import jax
import jax.numpy as jnp
from jax import lax
from jax.experimental import pallas as pl
from jax.experimental.pallas import tpu as pltpu
from jax.sharding import PartitionSpec as P

HEAD = 128
GROUP = 4
WIDTH_Q = GROUP * HEAD
WIDTH = WIDTH_Q + 2 * HEAD
PARTS = 8
ROWS = 384
OWN = ROWS // PARTS
RANK = 512
PANEL = 256
M_OWN = RANK // PARTS
G_OWN = HEAD // PARTS
BF16 = jnp.bfloat16
F32 = jnp.float32
MIB = 1024 * 1024
LIMIT0 = 56

QKV_ROWS = OWN * (WIDTH // HEAD)
M_AT = QKV_ROWS
G_AT = M_AT + M_OWN * (RANK // HEAD)
G_BLOCKS = ((0, 0), (0, 1), (1, 1), (2, 2), (2, 3), (3, 3), (0, 2), (0, 3), (1, 2), (1, 3))
MIXED_ROWS = G_AT + len(G_BLOCKS) * G_OWN
TAIL = 16

VMEM = pl.BlockSpec(memory_space=pltpu.VMEM)
SMEM = pl.BlockSpec(memory_space=pltpu.SMEM)
ANY = pl.BlockSpec(memory_space=pl.ANY)
HBM = pl.BlockSpec(memory_space=pltpu.HBM)


def call(body, name, out_shape, in_specs, flops, moved, args, scratch=(), out_specs=VMEM, limit=16):
    return pl.pallas_call(
        body,
        name=name,
        out_shape=out_shape,
        in_specs=in_specs,
        out_specs=out_specs,
        scratch_shapes=scratch,
        cost_estimate=pl.CostEstimate(flops=flops, bytes_accessed=moved, transcendentals=0),
        compiler_params=pltpu.CompilerParams(vmem_limit_bytes=limit * MIB),
    )(*args)


def dot(a, b):
    return jnp.dot(a, b, preferred_element_type=F32)


def dot_t(a, b):
    return lax.dot_general(a, b, (((1,), (1,)), ((), ())), preferred_element_type=F32)


def column_to_row(column):
    shape = (column.shape[0], HEAD)
    row = lax.broadcasted_iota(jnp.int32, shape, 0)
    lane = lax.broadcasted_iota(jnp.int32, shape, 1)
    return jnp.sum(jnp.where(row == lane, column, 0.0), axis=0, keepdims=True)


def row_to_column(row_vector, rows):
    row = lax.broadcasted_iota(jnp.int32, (rows, HEAD), 0)
    lane = lax.broadcasted_iota(jnp.int32, (rows, HEAD), 1)
    return jnp.sum(jnp.where(row == lane, row_vector, 0.0), axis=1, keepdims=True)


def pack(out, value, at, rows):
    for column in range(value.shape[1] // HEAD):
        part = value[:, column * HEAD : (column + 1) * HEAD]
        for to in range(PARTS):
            out[to, at + column * rows : at + (column + 1) * rows, :] = part[
                to * rows : (to + 1) * rows
            ]


def unpack(packed, at, rows, columns=1):
    parts = [
        packed[:, at + column * rows : at + (column + 1) * rows, :].reshape(PARTS * rows, HEAD)
        for column in range(columns)
    ]
    return parts[0] if columns == 1 else jnp.concatenate(parts, axis=1)


def qkv_sums(stream, squares, gain, weights, ready, buffer):
    tail_at = buffer.shape[1] - TAIL
    scaled = (stream * gain.astype(F32)).astype(BF16)
    row = lax.broadcasted_iota(jnp.int32, (TAIL, HEAD), 0)
    for to in range(PARTS):
        laid = column_to_row(squares[to * OWN : (to + 1) * OWN])
        high = laid.astype(BF16).astype(F32)
        value = jnp.where(row == 0, high, jnp.where(row == 1, laid - high, 0.0))
        buffer[to, tail_at:, :] = value.astype(BF16)
    ready()
    w_q, w_kv = weights
    for panel in range(WIDTH // PANEL):
        if panel < WIDTH_Q // PANEL:
            weight = w_q[:, panel * PANEL : (panel + 1) * PANEL]
        else:
            weight = w_kv[...]
        pack(buffer, dot(scaled, weight).astype(BF16), panel * OWN * (PANEL // HEAD), OWN)


def rotary_tables(lengths, tables):
    lane = lax.broadcasted_iota(jnp.int32, (OWN, HEAD), 1)
    half = HEAD // 2
    pair = jnp.where(lane < half, lane, lane - half).astype(F32)
    frequency = jnp.exp(pair * (-math.log(500000.0) / half))
    index = lax.broadcasted_iota(jnp.int32, (OWN, HEAD), 0) + lax.axis_index("tensor") * OWN
    for step in range(2):
        end, begin = 0, jnp.zeros((OWN, HEAD), jnp.int32)
        for document in range(3):
            end = end + lengths[0, step, document]
            begin = jnp.where(index >= end, end, begin)
        angle = (index - begin).astype(F32) * frequency
        sine = jnp.sin(angle)
        tables[2 * step] = jnp.cos(angle)
        tables[2 * step + 1] = jnp.where(lane < half, -sine, sine)


def symmetric_sums(basis, buffer):
    left, right = basis[:, :PANEL], basis[:, PANEL:]
    turned = left.T
    parts = {
        (0, 0): dot(turned, left).astype(BF16),
        (0, 2): dot(turned, right).astype(BF16),
        (2, 2): dot(right.T, right).astype(BF16),
    }
    for place, (row, column) in enumerate(G_BLOCKS):
        part = parts[(row // 2 * 2, column // 2 * 2)]
        row, column = row % 2 * HEAD, column % 2 * HEAD
        block = part[row : row + HEAD, column : column + HEAD]
        pack(buffer, block, G_AT + place * G_OWN, G_OWN)


def symmetric_blocks(packed):
    blocks = {
        pair: unpack(packed, G_AT + place * G_OWN, G_OWN) for place, pair in enumerate(G_BLOCKS)
    }

    def part(row, column):
        corner = (
            blocks[(row + 1, column)] if row != column else blocks[(row, column + 1)].T
        )
        upper = jnp.concatenate([blocks[(row, column)], blocks[(row, column + 1)]], axis=1)
        lower = jnp.concatenate([corner, blocks[(row + 1, column + 1)]], axis=1)
        return jnp.concatenate([upper, lower], axis=0)

    return part(0, 0), part(0, 2), part(2, 2)


def project0_kernel(
    lengths_in, basis_in, wo_in, coef_in, emb_in, gain_in, wq_in, wkv_in, out, tables,
    lengths, basis, w_o, coef, emb, gain, w_q, w_kv, sems,
):
    pairs = [
        (lengths_in, lengths), (basis_in, basis), (wo_in, w_o), (coef_in, coef),
        (emb_in.at[0, 0], emb), (gain_in, gain), (wq_in, w_q), (wkv_in, w_kv),
    ]
    copies = [
        pltpu.make_async_copy(source, target, sems.at[i])
        for i, (source, target) in enumerate(pairs)
    ]
    for copy in copies[:3]:
        copy.start()
    copies[0].wait()
    for copy in copies[3:]:
        copy.start()
    rotary_tables(lengths, tables)
    copies[1].wait()
    copies[2].wait()
    pack(out, dot(w_o[...], basis[...]).astype(BF16), M_AT, M_OWN)
    symmetric_sums(basis, out)
    for copy in copies[3:6]:
        copy.wait()
    stream = emb[...].astype(F32) + dot_t(coef[...], basis[...])
    squares = jnp.sum(stream * stream, axis=-1, keepdims=True)

    def ready():
        for copy in copies[6:]:
            copy.wait()

    qkv_sums(stream, squares, gain[...], (w_q, w_kv), ready, out)


def project1_kernel(coef_a, coef_b, gain, basis, emb, w_q, w_kv, out):
    coef = coef_a[...] + coef_b[...]
    stream = emb[0, 1].astype(F32) + dot_t(coef, basis[...])
    squares = jnp.sum(stream * stream, axis=-1, keepdims=True)
    qkv_sums(stream, squares, gain[...], (w_q, w_kv), lambda: None, out)


def turn(value, cosine, sine):
    return value * cosine + pltpu.roll(value, HEAD // 2, 1) * sine


def finish_kernel(width, step, parts, tables, out):
    def total(at, rows):
        value = parts[0, at : at + rows, :].astype(F32)
        for source in range(1, PARTS):
            value += parts[source, at : at + rows, :].astype(F32)
        return value

    for at in range(QKV_ROWS, out.shape[1], 16):
        value = total(at, 16).astype(BF16)
        for to in range(PARTS):
            out[to, at : at + 16, :] = value
    cosine, sine = tables[2 * step], tables[2 * step + 1]
    tail = total(parts.shape[1] - TAIL, TAIL)
    squares = row_to_column(tail[0:1] + tail[1:2], OWN)
    inverse = lax.rsqrt(squares * (1.0 / width) + 1e-05)
    for head in range(WIDTH // HEAD):
        rows = slice(head * OWN, (head + 1) * OWN)
        value = total(head * OWN, OWN) * inverse
        if head <= GROUP:
            value = turn(value, cosine, sine)
        value = value.astype(BF16)
        for to in range(PARTS):
            out[to, rows, :] = value


def attention(gathered, lengths, attended, after):
    first = lengths[0]
    second = first + lengths[1]
    third = second + lengths[2]
    heads = [unpack(gathered, head * OWN, OWN) for head in range(WIDTH // HEAD)]
    for tile in range(ROWS // HEAD):
        at = tile * HEAD
        count = at + HEAD
        queries = jnp.concatenate([heads[h][at:count] for h in range(GROUP)], axis=0)
        keys = heads[GROUP][:count]
        values = jnp.concatenate([heads[GROUP + 1][:count], jnp.ones((count, HEAD), BF16)], axis=1)
        row = lax.broadcasted_iota(jnp.int32, (HEAD, count), 0) + at
        column = lax.broadcasted_iota(jnp.int32, (HEAD, count), 1)
        begin = jnp.where(row >= first, first, 0)
        begin = jnp.where(row >= second, second, begin)
        begin = jnp.where(row >= third, third, begin)
        allowed = (column >= begin) & (column <= row)
        scores = dot_t(queries, keys) * HEAD ** (-0.5)
        for h in range(GROUP):
            own = jnp.where(allowed, scores[h * HEAD : (h + 1) * HEAD], -1e30)
            weights = jnp.exp(own - jnp.max(own, axis=-1, keepdims=True)).astype(BF16)
            summed = dot(weights, values)
            attended[at:count, h * HEAD : (h + 1) * HEAD] = (
                summed[:, :HEAD] / summed[:, HEAD:]
            ).astype(BF16)
        after(slice(at, count))


def carried_panels(coef, mixed):
    first, second = coef[:, :PANEL], coef[:, PANEL:]
    upper, cross, lower = symmetric_blocks(mixed)
    return dot(first, upper) + dot_t(second, cross), dot(first, cross) + dot(second, lower)


def boundary_tile(carried, attended, mixed, rows):
    columns = PANEL // HEAD
    return [
        (
            carried[panel][rows]
            + dot(
                attended[rows, :], unpack(mixed, M_AT + panel * columns * M_OWN, M_OWN, columns)
            )
        ).astype(BF16)
        for panel in range(RANK // PANEL)
    ]


def first_kernel(parity, gathered, coef, lengths_in, out, attended, lengths, sem):
    @pl.when(lax.axis_index("section") % 2 == parity)
    def _():
        copy = pltpu.make_async_copy(lengths_in, lengths, sem)
        copy.start()
        carried = carried_panels(coef[...], gathered)
        copy.wait()

        def after(rows):
            for panel, value in enumerate(boundary_tile(carried, attended, gathered, rows)):
                out[rows, panel * PANEL : (panel + 1) * PANEL] = value

        attention(gathered, [lengths[0, 0, i] for i in range(3)], attended, after)


def second_kernel(
    gathered, mixed, coef_a, coef_b, before_odd, before_even, lengths_in, out,
    attended, buffer, lengths, sems,
):
    lengths_copy = pltpu.make_async_copy(lengths_in, lengths, sems.at[3])
    lengths_copy.start()
    odd = lax.axis_index("section") % 2 == 1
    from_odd = pltpu.make_async_copy(before_odd, out.at[0], sems.at[0])
    from_even = pltpu.make_async_copy(before_even, out.at[0], sems.at[4])
    pl.when(odd)(from_odd.start)
    pl.when(jnp.logical_not(odd))(from_even.start)
    copies = []
    carried = carried_panels(coef_a[...] + coef_b[...], mixed)
    lengths_copy.wait()

    def after(rows):
        for panel, value in enumerate(boundary_tile(carried, attended, mixed, rows)):
            buffer[rows, panel * PANEL : (panel + 1) * PANEL] = value
        place = pl.ds(rows.start, HEAD)
        copy = pltpu.make_async_copy(
            buffer.at[place], out.at[1, place], sems.at[(1, 2, 5)[len(copies)]]
        )
        copy.start()
        copies.append(copy)

    attention(gathered, [lengths[0, 1, i] for i in range(3)], attended, after)
    for copy in copies:
        copy.wait()
    pl.when(odd)(from_odd.wait)
    pl.when(jnp.logical_not(odd))(from_even.wait)


def exchange(blocks):
    return lax.all_to_all(blocks, "tensor", 0, 0)


def hop(value, parity):
    sections = lax.axis_size("section")
    pairs = [(s, s + 1) for s in range(sections - 1) if s % 2 == parity]
    return lax.ppermute(value, "section", pairs)


def local(state_coef, embed_terms, norm_gain, w_query, w_keyval, w_out, basis, doc_lengths):
    w_q, w_kv, w_o = w_query[0], w_keyval[0], w_out[0]
    depth = embed_terms.shape[-1]
    width = depth * PARTS
    shape = jax.ShapeDtypeStruct
    flops, moved = 2 * ROWS * depth * (RANK + WIDTH), 5 * MIB

    def finish(step, sent, tables, rows):
        return call(
            functools.partial(finish_kernel, width, step), f"finish{step}",
            shape((PARTS, rows, HEAD), BF16), [VMEM] * 2,
            16 * rows * HEAD, 3 * MIB, (exchange(sent), tables),
        )

    coef0 = state_coef[0]
    args = (doc_lengths, basis, w_o, coef0, embed_terms, norm_gain, w_q, w_kv)
    held = [pltpu.VMEM(arg.shape, BF16) for arg in args]
    held[0] = pltpu.SMEM(doc_lengths.shape, jnp.int32)
    held[4] = pltpu.VMEM((ROWS, depth), BF16)
    sent0, tables = call(
        project0_kernel, "project0",
        (pltpu.VMEM((PARTS, MIXED_ROWS + TAIL, HEAD), BF16), pltpu.VMEM((4, OWN, HEAD), F32)),
        [ANY] * len(args), 2 * flops, moved, args,
        held + [pltpu.SemaphoreType.DMA((len(args),))], (VMEM, VMEM), LIMIT0,
    )
    mixed = exchange(finish(0, sent0, tables, MIXED_ROWS))
    attended = pltpu.VMEM((ROWS, WIDTH_Q), BF16)
    lengths = pltpu.SMEM(doc_lengths.shape, jnp.int32)
    attend_flops = 4 * ROWS * (ROWS * WIDTH_Q + RANK * RANK)
    step0 = (mixed, coef0, doc_lengths)
    boundary_even = call(
        functools.partial(first_kernel, 0), "attend0_even", shape((ROWS, RANK), BF16),
        [VMEM] * 2 + [ANY], attend_flops, 3 * MIB, step0,
        [attended, lengths, pltpu.SemaphoreType.DMA(())],
    )
    coef1_odd = hop(boundary_even, 0)
    boundary_odd = call(
        functools.partial(first_kernel, 1), "attend0_odd", shape((ROWS, RANK), BF16),
        [VMEM] * 2 + [ANY], attend_flops, 3 * MIB, step0,
        [attended, lengths, pltpu.SemaphoreType.DMA(())],
    )
    coef1 = (hop(boundary_odd, 1), coef1_odd)
    args = (*coef1, norm_gain, basis, embed_terms, w_q, w_kv)
    sent1 = call(
        project1_kernel, "project1", shape((PARTS, QKV_ROWS + TAIL, HEAD), BF16),
        [VMEM] * len(args), flops, moved, args,
    )
    heads = exchange(finish(1, sent1, tables, QKV_ROWS))
    both = call(
        second_kernel, "attend1", shape((2, ROWS, RANK), BF16), [VMEM] * 6 + [ANY],
        attend_flops, 4 * MIB,
        (heads, mixed, *coef1, boundary_odd, boundary_even, doc_lengths),
        [attended, pltpu.VMEM((ROWS, RANK), BF16), lengths, pltpu.SemaphoreType.DMA((6,))], HBM,
    )
    return both[None]


def solution(mesh):
    return jax.shard_map(
        local,
        mesh=mesh,
        in_specs=(
            P("section", None, None),
            P("section", None, None, "tensor"),
            P("section", "tensor"),
            P("section", "tensor", None),
            P("section", "tensor", None),
            P("section", None, "tensor"),
            P("tensor", None),
            P("section", None, None),
        ),
        out_specs=P("section", None, None, None),
        check_vma=False,
    )
```
